512 devices in a mesh: row: 64 (over y, x, core), rep: 8 (over z).
Axes of the slice: x: 4, y: 8, z: 8, core: 2. Of those that a mesh axis runs over, the one named last changes fastest.
Arguments:
- features: bfloat16 [32768, 768], P('row'), may hold values from -6 to 6
- order: int32 [32768], P('row'), may hold values from 0 to 32767, as said below
- adj_values: bfloat16 [256, 64, 3, 128, 128], P('row', 'rep'), may hold values from 0 to 0.044189453
- adj_cols: int32 [256, 64, 3], P('row', 'rep'), may hold values from 0 to 3, as said below
- adj_count: int32 [256, 64], P('row', 'rep'), may hold values from 0 to 3, as said below
- weight: bfloat16 [768, 1024], P(None, 'rep'), may hold values from -0.21875 to 0.21875
Outputs:
- hidden_out: bfloat16 [32768, 1024], P(('row', 'rep'))
The draws below stay inside these ranges and needn't reach their ends.
Inputs may be any that keep to these rules, and one draw needn't show every extreme that they name: order[n] lies in the same slab of 512 nodes as n; each slab's entries are a permutation of that slab. `adj_cols`: the 3 entries of one row block and source slab are different block indices. `adj_count`: every row block has 3 live slots for its own slab; some source slabs have none.
All inputs are finite; a program needn't handle non-finite values.
Results may differ from the reference program's by a relative error of at most 0.0049.
Values may be sent and summed in bfloat16 or wider, within the bound.
A program may use at most 128 MiB of HBM per device.

```python
import jax
import jax.numpy as jnp
from jax import lax

D_IN = 768
HID = 1024
BLK = 128
RB = 4
KB = 3
SLAB = 512
NODES = 32768
NRB = 256
N_ROW = 64


def slab_permutation(subkey):
    return jax.random.permutation(subkey, SLAB)


def block_choice(subkey):
    return jax.random.permutation(subkey, RB)[:KB]


def draw_order(key, part):
    key = jax.random.fold_in(key, 11)
    subkeys = jax.random.split(key, NODES // SLAB)
    perms = jax.vmap(slab_permutation)(subkeys).astype(jnp.int32)
    starts = (jnp.arange(NODES // SLAB, dtype=jnp.int32) * SLAB)[:, None]
    return (perms + starts).reshape(NODES)


def draw_adj_cols(key, part):
    key = jax.random.fold_in(key, 12)
    subkeys = jax.random.split(key, NRB * N_ROW)
    picked = jax.vmap(block_choice)(subkeys).astype(jnp.int32)
    return picked.reshape(NRB, N_ROW, KB)


def draw_adj_count(key, part):
    key = jax.random.fold_in(key, 13)
    first_key, second_key, third_key = jax.random.split(key, 3)
    counts = jax.random.randint(first_key, (NRB, N_ROW), 1, KB + 1, dtype=jnp.int32)
    picks = jax.random.randint(third_key, (NRB, N_ROW), 0, N_ROW, dtype=jnp.int32)
    counts = jnp.where(picks < 3 * N_ROW // 4, counts, 0)
    hottest = jax.random.randint(second_key, (NRB, 1), 0, N_ROW, dtype=jnp.int32)
    columns = jnp.arange(N_ROW, dtype=jnp.int32)[None, :]
    own_slab = (jnp.arange(NRB, dtype=jnp.int32) // RB)[:, None]
    counts = jnp.where(columns == hottest, KB, counts)
    return jnp.where(columns == own_slab, KB, counts).astype(jnp.int32)


def block_scale(stream_key, shape, pieces, low, largest):
    level, own = 1.0, jax.random.fold_in(stream_key, 6)
    for dim, shards_of in pieces:
        heights = jnp.exp(jax.random.uniform(jax.random.fold_in(own, dim), (shards_of,), jnp.float32, low / len(pieces), largest / len(pieces)))
        level = level * jnp.repeat(heights, shape[dim] // shards_of).reshape([-1 if axis == dim else 1 for axis in range(len(shape))])
    return level


def centred(stream_key, shape, spread, most, cuts=(), held_as=jnp.bfloat16):
    drawn = spread * jax.random.normal(stream_key, shape, jnp.float32)
    if cuts:
        drawn = drawn * block_scale(stream_key, shape, cuts, -0.22, 0.18)
    return jnp.clip(drawn, -most, most).astype(held_as)


def setup_inputs(seed: int = 0) -> dict:
    keys = jax.random.split(jax.random.key(seed), 7)
    return {
        "features": centred(keys[0], (NODES, D_IN), 1.0, 6.0, ((0, 64),)),
        "order": draw_order(jax.random.fold_in(keys[6], 71), 0),
        "adj_values": jnp.clip(0.044189453 * jax.random.uniform(keys[2], (NRB, N_ROW, KB, BLK, BLK), jnp.float32) ** block_scale(keys[2], (NRB, N_ROW, KB, BLK, BLK), ((0, 64), (1, 8)), -0.2, 0.2), 0.0, 0.044189453).astype(jnp.bfloat16),
        "adj_cols": draw_adj_cols(jax.random.fold_in(keys[6], 71), 0),
        "adj_count": draw_adj_count(jax.random.fold_in(keys[6], 71), 0),
        "weight": centred(keys[5], (D_IN, HID), D_IN ** -0.5, 0.21875, ((1, 8),)),
    }


def reference(features, order, adj_values, adj_cols, adj_count, weight):
    reordered = features[order]
    slab_blocks = reordered.reshape(N_ROW, RB, BLK, D_IN)
    live_slots = (jnp.arange(KB, dtype=jnp.int32)[None, None, :] < adj_count[:, :, None]).astype(jnp.float32)
    sources = jnp.arange(N_ROW, dtype=jnp.int32)[:, None]

    def block_row(inputs):
        values, columns, weights_live = inputs
        chosen = slab_blocks[sources, columns].astype(jnp.float32)
        scaled = values.astype(jnp.float32) * weights_live[:, :, None, None]
        return jnp.einsum("skij,skjd->id", scaled, chosen)

    aggregated_r = lax.map(block_row, (adj_values, adj_cols, live_slots)).reshape(NODES, D_IN)
    aggregated = jnp.zeros_like(aggregated_r).at[order].set(aggregated_r)
    rounded = aggregated.astype(jnp.bfloat16)
    product = jnp.dot(rounded, weight, preferred_element_type=jnp.float32)
    return jax.nn.relu(product).astype(jnp.bfloat16)
```

```python
import functools

import jax
import jax.numpy as jnp
from jax import lax
from jax.experimental import pallas as pl
from jax.experimental.pallas import tpu as pltpu
from jax.sharding import PartitionSpec as P

MESH = pl.DeviceIdType.MESH
NY, NX, NC, NZ = 8, 4, 2, 8
BLK = 128
RB = 4
KB = 3
SLAB = RB * BLK
CHUNKS = 6
STEPS = CHUNKS * RB
LAG_X1 = 4
LAG_X2 = 8
LAG_COMPUTE = 12
LAG_WEIGHT = 14
LAG_FINAL = 24
ITERS = 4 * (CHUNKS - 1) + LAG_FINAL + 1
YP1, YM1, YP2, YM2, XP, XM, FR, FL, SIB = range(9)
KINDS = SIB + NX


def kernel(
    feat_hbm, order_ref, adj_hbm, cols_ref, count_ref, w_hbm, out_ref,
    slabs, adj, raw, dense, feat, perm, w_own, w_all, part, z_out, z_in, total,
    load_sem, send_sem, recv_sem, sib_sem, z_send, z_recv, w_send, w_recv, w_sib_send, w_sib_recv,
):
    row = lax.axis_index("row")
    rep = lax.axis_index("rep")
    c = row % NC
    x = (row // NC) % NX
    y = row // (NC * NX)
    d = (y - rep + NY) % NY

    def device(dy, dx, dc):
        return ((((y + dy) % NY) * NX + (x + dx) % NX) * NC + (c + dc) % NC, rep)

    left, right, sibling = device(0, NX - 1, 0), device(0, 1, 0), device(0, 0, 1)
    up1, down1, up2, down2 = device(1, 0, 0), device(NY - 1, 0, 0), device(2, 0, 0), device(NY - 2, 0, 0)

    barrier = pltpu.get_barrier_semaphore()
    for near in (left, right, sibling, up1, down1, up2, down2):
        pl.semaphore_signal(barrier, inc=1, device_id=near, device_id_type=MESH)
    for k in range(1, NZ):
        pl.semaphore_signal(barrier, inc=1, device_id=(row, (rep + k) % NZ), device_id_type=MESH)

    load_feat = pltpu.make_async_copy(feat_hbm, feat, load_sem.at[0])
    load_w = pltpu.make_async_copy(w_hbm, w_own, load_sem.at[1])
    load_adj = pltpu.make_async_copy(adj_hbm, adj.at[pl.ds(0, RB * NZ * KB)], load_sem.at[2])

    @pl.when(d == 0)
    def _():
        load_feat.start()

    load_w.start()
    load_adj.start()

    local = order_ref[...] - row * SLAB
    rows_of = lax.broadcasted_iota(jnp.int32, (SLAB, SLAB), 0)
    perm[...] = (rows_of == local).astype(jnp.float32).astype(jnp.bfloat16)
    adj[RB * NZ * KB] = jnp.zeros((BLK, BLK), jnp.bfloat16)
    total[...] = jnp.zeros_like(total)

    def unit(s, x0):
        return slabs.at[s // RB, c * NX + x0, pl.ds((s % RB) * BLK, BLK)]

    @pl.when(d == 0)
    def _():
        load_feat.wait()
        ordered = lax.dot_general(
            perm[...], feat[...], (((0,), (0,)), ((), ())), preferred_element_type=jnp.float32
        ).astype(jnp.bfloat16)
        for ch in range(CHUNKS):
            slabs[ch, c * NX + x] = ordered[:, ch * BLK:(ch + 1) * BLK]

    load_w.wait()
    half = CHUNKS // 2
    w_all[pl.ds(c * half, half), :, pl.ds(pl.multiple_of(rep * BLK, BLK), BLK)] = w_own[pl.ds(c * half, half)]
    pl.semaphore_wait(barrier, 7 + NZ - 1)

    def copy_to(s, x0, kind, target):
        ref = unit(s, x0)
        return pltpu.make_async_remote_copy(
            src_ref=ref, dst_ref=ref, send_sem=send_sem.at[kind, s], recv_sem=recv_sem.at[s, x0],
            device_id=target, device_id_type=MESH,
        )

    def copy_sib(s, x0, rel):
        ref = unit(s, x0)
        return pltpu.make_async_remote_copy(
            src_ref=ref, dst_ref=ref, send_sem=send_sem.at[SIB + rel, s], recv_sem=sib_sem.at[s // RB],
            device_id=sibling, device_id_type=MESH,
        )

    def y_sends(s):
        even = s % 2 == 0
        return (
            ((d == 0) | ((d == 2) & even), YP2, up2),
            ((d == 0) | ((d == NY - 2) & jnp.logical_not(even)), YM2, down2),
            ((d == 2) | (d == NY - 2), YP1, up1),
            ((d == 2) | (d == NY - 2), YM1, down1),
        )

    def w_copy(k):
        return pltpu.make_async_remote_copy(
            src_ref=w_own.at[pl.ds(c * half, half)],
            dst_ref=w_all.at[pl.ds(c * half, half), :, pl.ds(pl.multiple_of(rep * BLK, BLK), BLK)],
            send_sem=w_send.at[k - 1], recv_sem=w_recv,
            device_id=(row, (rep + k) % NZ), device_id_type=MESH,
        )

    def w_sib_copy():
        ref = w_all.at[pl.ds(c * half, half)]
        return pltpu.make_async_remote_copy(
            src_ref=ref, dst_ref=ref, send_sem=w_sib_send, recv_sem=w_sib_recv,
            device_id=sibling, device_id_type=MESH,
        )

    def z_copy(ch, k):
        peer = (rep + k) % NZ
        return pltpu.make_async_remote_copy(
            src_ref=z_out.at[ch, peer], dst_ref=z_in.at[ch, rep],
            send_sem=z_send.at[k - 1, ch], recv_sem=z_recv.at[ch],
            device_id=(row, peer), device_id_type=MESH,
        )

    Z_ORDER = (4, 3, 5, 2, 6, 1, 7)
    for k in Z_ORDER:
        w_copy(k).start()

    def iteration(i, carry):
        @pl.when(i < STEPS)
        def _():
            s = i

            @pl.when(d != 0)
            def _():
                copy_to(s, x, XP, right).wait_recv()

            for cond, kind, target in y_sends(s):
                @pl.when(cond)
                def _(kind=kind, target=target):
                    copy_to(s, x, kind, target).start()

            copy_to(s, x, XP, right).start()
            copy_to(s, x, XM, left).start()
            copy_sib(s, x, 0).start()

        @pl.when((i >= LAG_X1) & (i < STEPS + LAG_X1))
        def _():
            s = i - LAG_X1
            xl, xr = (x + NX - 1) % NX, (x + 1) % NX
            copy_to(s, xl, FR, right).wait_recv()

            @pl.when(s % 2 == 0)
            def _():
                copy_to(s, xl, FR, right).start()

            copy_sib(s, xl, 1).start()
            copy_to(s, xr, FL, left).wait_recv()

            @pl.when(s % 2 == 1)
            def _():
                copy_to(s, xr, FL, left).start()

            copy_sib(s, xr, 3).start()

        @pl.when((i >= LAG_X2) & (i < STEPS + LAG_X2))
        def _():
            s = i - LAG_X2
            xo = (x + 2) % NX
            copy_to(s, xo, FR, right).wait_recv()
            copy_sib(s, xo, 2).start()

        @pl.when(i == 0)
        def _():
            load_adj.wait()

        @pl.when(i < 2 * NX)
        def _():
            jj = i
            j = (jj % NX) * NC + jj // NX
            for b in range(RB):
                cols = [cols_ref[k, b, j] for k in range(KB)]
                n = count_ref[b, j]
                base = (b * NZ + j) * KB
                for cb in range(RB):
                    index = jnp.int32(RB * NZ * KB)
                    for k in range(KB):
                        index = jnp.where((n > k) & (cols[k] == cb), base + k, index)
                    raw[b * BLK:(b + 1) * BLK, cb * BLK:(cb + 1) * BLK] = adj[index]
            dense[jj] = jnp.dot(
                perm[...], raw[...], preferred_element_type=jnp.float32
            ).astype(jnp.bfloat16)

        at = i - LAG_COMPUTE

        @pl.when((at >= 0) & (at < STEPS))
        def _():
            ch = at // RB
            q = at % RB

            @pl.when(q == 2)
            def _():
                ref = slabs.at[ch, pl.ds((1 - c) * NX, NX)]
                pltpu.make_async_remote_copy(
                    src_ref=ref, dst_ref=ref, send_sem=send_sem.at[SIB, 0], recv_sem=sib_sem.at[ch],
                    device_id=sibling, device_id_type=MESH,
                ).wait_recv()

            layer = jnp.where(q < 2, c, 1 - c)
            first = layer * NX + (q % 2) * 2
            update = jnp.dot(dense[first], slabs[ch, first], preferred_element_type=jnp.float32) + jnp.dot(
                dense[first + 1], slabs[ch, first + 1], preferred_element_type=jnp.float32
            )

            @pl.when(q == 0)
            def _():
                part[...] = update

            @pl.when(q > 0)
            def _():
                part[...] += update

            @pl.when(q == RB - 1)
            def _():
                z_out[ch] = part[...].astype(jnp.bfloat16).reshape(NZ, SLAB // NZ, BLK)
                for k in Z_ORDER:
                    z_copy(ch, k).start()
                z_in[ch, rep] = z_out[ch, rep]

        @pl.when(i == LAG_WEIGHT)
        def _():
            ref = w_all.at[pl.ds(c * half, half), :, pl.ds(0, (NZ - 1) * BLK)]
            pltpu.make_async_remote_copy(
                src_ref=ref, dst_ref=ref, send_sem=w_sib_send, recv_sem=w_recv,
                device_id=sibling, device_id_type=MESH,
            ).wait_recv()
            w_sib_copy().start()

        @pl.when(i == LAG_FINAL - 1)
        def _():
            ref = w_all.at[pl.ds((1 - c) * half, half)]
            pltpu.make_async_remote_copy(
                src_ref=ref, dst_ref=ref, send_sem=w_sib_send, recv_sem=w_sib_recv,
                device_id=sibling, device_id_type=MESH,
            ).wait_recv()

        last = i - LAG_FINAL

        @pl.when((last >= 0) & (last % RB == 0))
        def _():
            ch = last // RB

            @pl.when(ch == CHUNKS - 1)
            def _():
                def sent(s, carry):
                    for cond, kind, target in y_sends(s):
                        @pl.when(cond)
                        def _(kind=kind, target=target):
                            copy_to(s, x, kind, target).wait_send()
                    copy_to(s, x, XP, right).wait_send()
                    copy_to(s, x, XM, left).wait_send()

                    @pl.when(s % 2 == 0)
                    def _():
                        copy_to(s, (x + NX - 1) % NX, FR, right).wait_send()

                    @pl.when(s % 2 == 1)
                    def _():
                        copy_to(s, (x + 1) % NX, FL, left).wait_send()

                    for rel in range(NX):
                        copy_sib(s, x, rel).wait_send()
                    return carry

                lax.fori_loop(0, STEPS, sent, 0)
                w_sib_copy().wait_send()
                for k in Z_ORDER:
                    w_copy(k).wait_send()

            ref = z_in.at[ch, pl.ds(0, NZ - 1)]
            pltpu.make_async_remote_copy(
                src_ref=ref, dst_ref=ref, send_sem=w_sib_send, recv_sem=z_recv.at[ch],
                device_id=sibling, device_id_type=MESH,
            ).wait_recv()
            rounded = jnp.sum(z_in[ch].astype(jnp.float32), axis=0).astype(jnp.bfloat16)
            total[...] += jnp.dot(rounded, w_all[ch], preferred_element_type=jnp.float32)

        return carry

    lax.fori_loop(0, ITERS, iteration, 0)
    out_ref[...] = jnp.maximum(total[...], 0.0).astype(jnp.bfloat16)

    def z_sent(ch, carry):
        for k in Z_ORDER:
            z_copy(ch, k).wait_send()
        return carry

    lax.fori_loop(0, CHUNKS, z_sent, 0)


def shards(features, order, adj_values, adj_cols, adj_count, weight):
    hid = NZ * BLK
    bf16, f32 = jnp.bfloat16, jnp.float32
    dma = pltpu.SemaphoreType.DMA
    any_space = pl.BlockSpec(memory_space=pl.ANY)
    return pl.pallas_call(
        kernel,
        out_shape=jax.ShapeDtypeStruct((SLAB // NZ, hid), bf16),
        in_specs=[
            any_space,
            pl.BlockSpec(memory_space=pltpu.VMEM),
            any_space,
            pl.BlockSpec(memory_space=pltpu.SMEM),
            pl.BlockSpec(memory_space=pltpu.SMEM),
            any_space,
        ],
        out_specs=pl.BlockSpec(memory_space=pltpu.VMEM),
        scratch_shapes=[
            pltpu.VMEM((CHUNKS, NC * NX, SLAB, BLK), bf16),
            pltpu.VMEM((RB * NZ * KB + 1, BLK, BLK), bf16),
            pltpu.VMEM((SLAB, SLAB), bf16),
            pltpu.VMEM((NC * NX, SLAB, SLAB), bf16),
            pltpu.VMEM((SLAB, CHUNKS * BLK), bf16),
            pltpu.VMEM((SLAB, SLAB), bf16),
            pltpu.VMEM((CHUNKS, BLK, BLK), bf16),
            pltpu.VMEM((CHUNKS, BLK, hid), bf16),
            pltpu.VMEM((SLAB, BLK), f32),
            pltpu.VMEM((CHUNKS, NZ, SLAB // NZ, BLK), bf16),
            pltpu.VMEM((CHUNKS, NZ, SLAB // NZ, BLK), bf16),
            pltpu.VMEM((SLAB // NZ, hid), f32),
            dma((3,)),
            dma((KINDS, STEPS)),
            dma((STEPS, NX)),
            dma((CHUNKS,)),
            dma((NZ - 1, CHUNKS)),
            dma((CHUNKS,)),
            dma((NZ - 1,)),
            dma,
            dma,
            dma,
        ],
        compiler_params=pltpu.CompilerParams(
            collective_id=0, has_side_effects=True, vmem_limit_bytes=56 << 20
        ),
    )(
        features,
        order.reshape(1, SLAB),
        adj_values.reshape(RB * NZ * KB, BLK, BLK),
        adj_cols.transpose(2, 0, 1),
        adj_count,
        weight.reshape(CHUNKS, BLK, BLK),
    )


def solution(mesh):
    placed = (
        P("row", None),
        P("row"),
        P("row", "rep", None, None, None),
        P("row", "rep", None),
        P("row", "rep"),
        P(None, "rep"),
    )
    return jax.shard_map(
        shards, mesh=mesh, in_specs=placed, out_specs=P(("row", "rep"), None), check_vma=False
    )
```

```python
import functools

import jax
import jax.numpy as jnp
from jax import lax
from jax.experimental import pallas as pl
from jax.experimental.pallas import tpu as pltpu
from jax.sharding import PartitionSpec as P

MESH = pl.DeviceIdType.MESH
NY, NX, NC, NZ = 8, 4, 2, 8
BLK = 128
RB = 4
KB = 3
SLAB = RB * BLK
CHUNKS = 6
SUB = 4
ROWS = SLAB // SUB
STEPS = CHUNKS * SUB
PRE = 6
LAG_X1 = 4
LAG_X2 = 8
LAG_COMPUTE = 12
ITERS = LAG_X2 + STEPS
DIRECT = STEPS - SUB
READY_AT = 4
WEIGHT_AT = 22
YP1, YM1, YP2, YM2, XP, XM, XO, FR, FL, SIB = range(10)
KINDS = SIB + 1


def kernel(
    feat_hbm, order_hbm, adj_hbm, cols_hbm, count_hbm, w_hbm, out_ref,
    slabs, adj, dense, feat, perm, order, cols_ref, count_ref, w_all, part, z_out, z_in, total,
    load_sem, send_sem, recv_sem, sib_sem, z_send, z_recv, w_send, w_recv, w_sib_send, w_sib_recv, ready,
):
    row = lax.axis_index("row")
    rep = lax.axis_index("rep")
    c = row % NC
    x = (row // NC) % NX
    y = row // (NC * NX)
    d = (y - rep + NY) % NY

    def device(dy, dx, dc):
        return ((((y + dy) % NY) * NX + (x + dx) % NX) * NC + (c + dc) % NC, rep)

    left, right, opposite, sibling = device(0, NX - 1, 0), device(0, 1, 0), device(0, 2, 0), device(0, 0, 1)
    up1, down1, up2, down2 = device(1, 0, 0), device(NY - 1, 0, 0), device(2, 0, 0), device(NY - 2, 0, 0)

    barrier = pltpu.get_barrier_semaphore()
    near = (left, right, opposite, sibling, up1, down1, up2, down2)
    for other in near:
        pl.semaphore_signal(barrier, inc=1, device_id=other, device_id_type=MESH)
    for k in range(1, NZ):
        @pl.when(rep + k < NZ)
        def _(k=k):
            pl.semaphore_signal(barrier, inc=1, device_id=(row, rep + k), device_id_type=MESH)

    load_order = pltpu.make_async_copy(order_hbm, order, load_sem.at[0])
    load_feat = pltpu.make_async_copy(feat_hbm, feat, load_sem.at[1])
    load_adj = pltpu.make_async_copy(adj_hbm, adj.at[pl.ds(0, RB * NZ * KB)], load_sem.at[2])
    load_cols = pltpu.make_async_copy(cols_hbm, cols_ref, load_sem.at[3])
    load_count = pltpu.make_async_copy(count_hbm, count_ref, load_sem.at[4])
    load_w = pltpu.make_async_copy(w_hbm, w_all.at[rep], load_sem.at[5])
    load_order.start()

    @pl.when(d == 0)
    def _():
        load_feat.start()

    load_adj.start()
    load_cols.start()
    load_count.start()
    load_w.start()
    load_order.wait()
    local = order[...] - row * SLAB
    rows_of = lax.broadcasted_iota(jnp.int32, (SLAB, SLAB), 0)
    perm[...] = (rows_of == local).astype(jnp.float32).astype(jnp.bfloat16)

    def unit(s, x0):
        return slabs.at[s // SUB, c * NX + x0, pl.ds((s % SUB) * ROWS, ROWS)]

    @pl.when(d == 0)
    def _():
        load_feat.wait()
        ordered = lax.dot_general(
            perm[...], feat[...], (((0,), (0,)), ((), ())), preferred_element_type=jnp.float32
        ).astype(jnp.bfloat16)
        for ch in range(CHUNKS):
            slabs[ch, c * NX + x] = ordered[:, ch * BLK:(ch + 1) * BLK]

    pl.semaphore_wait(barrier, len(near) + rep)
    for k in range(1, NZ):
        @pl.when(rep >= k)
        def _(k=k):
            pl.semaphore_signal(ready, inc=1, device_id=(row, rep - k), device_id_type=MESH)

    def remote(src, dst, sent, landed, target):
        return pltpu.make_async_remote_copy(
            src_ref=src, dst_ref=dst, send_sem=sent, recv_sem=landed, device_id=target, device_id_type=MESH
        )

    def copy_to(s, x0, kind, target):
        return remote(unit(s, x0), unit(s, x0), send_sem.at[kind], recv_sem.at[s, x0], target)

    def copy_sib(s, x0):
        return remote(unit(s, x0), unit(s, x0), send_sem.at[SIB], sib_sem.at[s // SUB], sibling)

    second = (d == 2) | (d == NY - 2)

    half = CHUNKS // 2
    mine = pl.ds(c * half, half)

    def w_copy(k):
        ref = w_all.at[rep, mine]
        return remote(ref, ref, w_send, w_recv, (row, (rep + k) % NZ))

    def w_sib():
        ref = w_all.at[:, mine]
        return remote(ref, ref, w_sib_send, w_sib_recv, sibling)

    load_w.wait()
    for k in (4, 3, 5, 2, 6, 1, 7):
        pl.when(rep + k >= NZ)(w_copy(k).start)

    def own_step(s):
        even = s % 2 == 0
        for cond, kind, target in (
            ((d == 0) | ((d == 2) & even), YP2, up2),
            ((d == 0) | ((d == NY - 2) & jnp.logical_not(even)), YM2, down2),
            (second, YP1, up1),
            (second, YM1, down1),
        ):
            pl.when(cond)(copy_to(s, x, kind, target).start)
        copy_to(s, x, XP, right).start()
        copy_to(s, x, XM, left).start()
        pl.when(s >= DIRECT)(copy_to(s, x, XO, opposite).start)
        copy_sib(s, x).start()

    def arrive(s, x0):
        copy_to(s, x0, XP, right).wait_recv()

    def all_sent(kind, chunks):
        ref = slabs.at[pl.ds(0, chunks), 0]
        remote(ref, ref, send_sem.at[kind], w_recv, right).wait_send()

    def z_copy(ch, peer):
        return remote(z_out.at[ch, peer], z_in.at[ch, rep], z_send, z_recv.at[ch], (row, peer))

    @pl.when(d == 0)
    def _():
        def first(s, carry):
            own_step(s)
            return carry

        lax.fori_loop(0, PRE, first, 0)

    adj[RB * NZ * KB] = jnp.zeros((BLK, BLK), jnp.bfloat16)
    load_cols.wait()
    load_count.wait()
    load_adj.wait()

    def build(jj, carry):
        j = (jj % NX) * NC + jj // NX
        for b in range(RB):
            cols = [cols_ref[k, b, j] for k in range(KB)]
            n = count_ref[b, j]
            base = (b * NZ + j) * KB
            for cb in range(RB):
                index = jnp.int32(RB * NZ * KB)
                for k in range(KB):
                    index = jnp.where((n > k) & (cols[k] == cb), base + k, index)
                dense[jj, b * BLK:(b + 1) * BLK, cb * BLK:(cb + 1) * BLK] = adj[index]
        return carry

    lax.fori_loop(0, NC * NX, build, 0)
    total[...] = jnp.zeros_like(total)

    def product(m, carry):
        ch, q = m // RB, m % RB

        @pl.when(q == 2)
        def _():
            ref = slabs.at[ch, pl.ds((1 - c) * NX, NX)]
            remote(ref, ref, w_sib_send, sib_sem.at[ch], sibling).wait_recv()

        layer = jnp.where(q < 2, c, 1 - c)
        first = layer * NX + (q % 2) * 2
        update = jnp.dot(dense[first], slabs[ch, first], preferred_element_type=jnp.float32) + jnp.dot(
            dense[first + 1], slabs[ch, first + 1], preferred_element_type=jnp.float32
        )

        @pl.when(q == 0)
        def _():
            part[...] = update

        @pl.when(q > 0)
        def _():
            part[...] += update

        @pl.when(q == RB - 1)
        def _():
            initial = jnp.dot(perm[...], part[...].astype(jnp.bfloat16), preferred_element_type=jnp.float32)
            z_out[ch] = initial.astype(jnp.bfloat16).reshape(NZ, SLAB // NZ, BLK)
            for peer in range(NZ):
                pl.when(rep != peer)(z_copy(ch, peer).start)
            z_in[ch, rep] = z_out[ch, rep]

        return carry

    def iteration(i, carry):
        now = i + jnp.where(d == 0, PRE, 0)

        @pl.when((d != 0) & (i < STEPS))
        def _():
            arrive(i, x)

        @pl.when(now < STEPS)
        def _():
            own_step(now)

        @pl.when((i >= LAG_X1) & (i < STEPS + LAG_X1))
        def _():
            s = i - LAG_X1
            forward = s < DIRECT
            to_right = s % 2 == 0
            from_left, from_right = (x + NX - 1) % NX, (x + 1) % NX
            arrive(s, from_left)
            pl.when(forward & to_right)(copy_to(s, from_left, FR, right).start)
            copy_sib(s, from_left).start()
            arrive(s, from_right)
            pl.when(forward & jnp.logical_not(to_right))(copy_to(s, from_right, FL, left).start)
            copy_sib(s, from_right).start()

        @pl.when(i >= LAG_X2)
        def _():
            arrive(i - LAG_X2, (x + 2) % NX)
            copy_sib(i - LAG_X2, (x + 2) % NX).start()

        @pl.when(i == READY_AT)
        def _():
            @pl.when(rep < NZ - 1)
            def _():
                pl.semaphore_wait(ready, NZ - 1 - rep)

            for k in (4, 3, 5, 2, 6, 1, 7):
                pl.when(rep + k < NZ)(w_copy(k).start)

        @pl.when(i == WEIGHT_AT)
        def _():
            ref = w_all.at[pl.ds(0, NZ - 1), mine]
            remote(ref, ref, w_send, w_recv, sibling).wait()
            w_sib().start()

        @pl.when((i >= LAG_COMPUTE) & (i < LAG_COMPUTE + (CHUNKS - 1) * SUB))
        def _():
            at = (i - LAG_COMPUTE) * (RB // SUB)
            lax.fori_loop(at, at + RB // SUB, product, 0)

        return carry

    lax.fori_loop(0, ITERS, iteration, 0)
    lax.fori_loop((CHUNKS - 1) * RB, CHUNKS * RB, product, 0)

    for kind in (XP, XM):
        all_sent(kind, CHUNKS)
    all_sent(XO, 1)
    for kind in (FR, FL):
        ref = slabs.at[0, pl.ds(0, CHUNKS - 1), pl.ds(0, SLAB // 2)]
        remote(ref, ref, send_sem.at[kind], w_recv, right).wait_send()
    ref = slabs.at[:, pl.ds(0, NX)]
    remote(ref, ref, send_sem.at[SIB], w_recv, right).wait_send()

    @pl.when(d == 0)
    def _():
        all_sent(YP2, CHUNKS)
        all_sent(YM2, CHUNKS)

    @pl.when(second)
    def _():
        all_sent(YP1, CHUNKS)
        all_sent(YM1, CHUNKS)

    pl.when(d == 2)(functools.partial(all_sent, YP2, CHUNKS // 2))
    pl.when(d == NY - 2)(functools.partial(all_sent, YM2, CHUNKS // 2))
    w_sib().wait()

    def finish(ch, carry):
        ref = z_in.at[ch, pl.ds(0, NZ - 1)]
        remote(ref, ref, w_sib_send, z_recv.at[ch], sibling).wait_recv()
        rounded = jnp.sum(z_in[ch].astype(jnp.float32), axis=0).astype(jnp.bfloat16)
        for k in range(NZ):
            total[:, k * BLK:(k + 1) * BLK] += jnp.dot(rounded, w_all[k, ch], preferred_element_type=jnp.float32)
        return carry

    lax.fori_loop(0, CHUNKS, finish, 0)
    out_ref[...] = jnp.maximum(total[...], 0.0).astype(jnp.bfloat16)
    ref = z_out.at[:, pl.ds(0, NZ - 1)]
    remote(ref, ref, z_send, w_sib_recv, sibling).wait_send()


def shards(features, order, adj_values, adj_cols, adj_count, weight):
    hid = NZ * BLK
    bf16, f32, i32 = jnp.bfloat16, jnp.float32, jnp.int32
    dma = pltpu.SemaphoreType.DMA
    return pl.pallas_call(
        kernel,
        out_shape=jax.ShapeDtypeStruct((SLAB // NZ, hid), bf16),
        in_specs=[pl.BlockSpec(memory_space=pl.ANY)] * 6,
        out_specs=pl.BlockSpec(memory_space=pltpu.VMEM),
        scratch_shapes=[
            pltpu.VMEM((CHUNKS, NC * NX, SLAB, BLK), bf16),
            pltpu.VMEM((RB * NZ * KB + 1, BLK, BLK), bf16),
            pltpu.VMEM((NC * NX, SLAB, SLAB), bf16),
            pltpu.VMEM((SLAB, CHUNKS * BLK), bf16),
            pltpu.VMEM((SLAB, SLAB), bf16),
            pltpu.VMEM((1, SLAB), i32),
            pltpu.SMEM((KB, RB, NZ), i32),
            pltpu.SMEM((RB, NZ), i32),
            pltpu.VMEM((NZ, CHUNKS, BLK, BLK), bf16),
            pltpu.VMEM((SLAB, BLK), f32),
            pltpu.VMEM((CHUNKS, NZ, SLAB // NZ, BLK), bf16),
            pltpu.VMEM((CHUNKS, NZ, SLAB // NZ, BLK), bf16),
            pltpu.VMEM((SLAB // NZ, hid), f32),
            dma((6,)),
            dma((KINDS,)),
            dma((STEPS, NX)),
            dma((CHUNKS,)),
            dma,
            dma((CHUNKS,)),
            dma,
            dma,
            dma,
            dma,
            pltpu.SemaphoreType.REGULAR,
        ],
        compiler_params=pltpu.CompilerParams(
            collective_id=0, has_side_effects=True, vmem_limit_bytes=56 << 20
        ),
    )(
        features,
        order.reshape(1, SLAB),
        adj_values.reshape(RB * NZ * KB, BLK, BLK),
        adj_cols.transpose(2, 0, 1),
        adj_count,
        weight.reshape(CHUNKS, BLK, BLK),
    )


def solution(mesh):
    placed = (
        P("row", None),
        P("row"),
        P("row", "rep", None, None, None),
        P("row", "rep", None),
        P("row", "rep"),
        P(None, "rep"),
    )
    return jax.shard_map(
        shards, mesh=mesh, in_specs=placed, out_specs=P(("row", "rep"), None), check_vma=False
    )
```

```python
import functools

import jax
import jax.numpy as jnp
from jax import lax
from jax.experimental import pallas as pl
from jax.experimental.pallas import tpu as pltpu
from jax.sharding import PartitionSpec as P

MESH = pl.DeviceIdType.MESH
NY, NX, NC, NZ = 8, 4, 2, 8
BLK = 128
RB = 4
KB = 3
SLAB = RB * BLK
CHUNKS = 6
SUB = 4
ROWS = SLAB // SUB
STEPS = CHUNKS * SUB
PRE = 4
LAG_X1 = 4
LAG_X2 = 8
LAG_COMPUTE = 10
ITERS = LAG_X2 + STEPS
DIRECT = STEPS - 1
READY_AT = 4
WEIGHT_AT = 22
YP1, YM1, YP2, YM2, XP, XM, XO, FR, FL, SIB = range(10)
KINDS = SIB + 1


def kernel(
    feat_hbm, order_hbm, adj_hbm, cols_hbm, count_hbm, w_hbm, out_ref,
    slabs, adj, dense, feat, perm, order, cols_ref, count_ref, w_all, part, z_out, z_in, total,
    load_sem, send_sem, recv_sem, sib_sem, z_send, z_recv, w_send, w_recv, w_sib_send, w_sib_recv, ready,
):
    row = lax.axis_index("row")
    rep = lax.axis_index("rep")
    c = row % NC
    x = (row // NC) % NX
    y = row // (NC * NX)
    d = (y - rep + NY) % NY

    def device(dy, dx, dc):
        return ((((y + dy) % NY) * NX + (x + dx) % NX) * NC + (c + dc) % NC, rep)

    left, right, opposite, sibling = device(0, NX - 1, 0), device(0, 1, 0), device(0, 2, 0), device(0, 0, 1)
    up1, down1, up2, down2 = device(1, 0, 0), device(NY - 1, 0, 0), device(2, 0, 0), device(NY - 2, 0, 0)

    barrier = pltpu.get_barrier_semaphore()
    near = (left, right, opposite, sibling, up1, down1, up2, down2)
    for other in near:
        pl.semaphore_signal(barrier, inc=1, device_id=other, device_id_type=MESH)
    for k in range(1, NZ):
        @pl.when(rep + k < NZ)
        def _(k=k):
            pl.semaphore_signal(barrier, inc=1, device_id=(row, rep + k), device_id_type=MESH)

    load_order = pltpu.make_async_copy(order_hbm, order, load_sem.at[0])
    load_feat = pltpu.make_async_copy(feat_hbm, feat, load_sem.at[1])
    load_adj = pltpu.make_async_copy(adj_hbm, adj.at[pl.ds(0, RB * NZ * KB)], load_sem.at[2])
    load_cols = pltpu.make_async_copy(cols_hbm, cols_ref, load_sem.at[3])
    load_count = pltpu.make_async_copy(count_hbm, count_ref, load_sem.at[4])
    load_w = pltpu.make_async_copy(w_hbm, w_all.at[rep], load_sem.at[5])
    load_order.start()

    @pl.when(d == 0)
    def _():
        load_feat.start()

    load_adj.start()
    load_cols.start()
    load_count.start()
    load_w.start()
    load_order.wait()
    local = order[...] - row * SLAB
    rows_of = lax.broadcasted_iota(jnp.int32, (SLAB, SLAB), 0)
    perm[...] = (rows_of == local).astype(jnp.float32).astype(jnp.bfloat16)

    def unit(s, x0):
        return slabs.at[s // SUB, c * NX + x0, pl.ds((s % SUB) * ROWS, ROWS)]

    def in_order(first, count):
        ordered = lax.dot_general(
            perm[...], feat[:, first * BLK:(first + count) * BLK], (((0,), (0,)), ((), ())),
            preferred_element_type=jnp.float32,
        ).astype(jnp.bfloat16)
        for k in range(count):
            slabs[first + k, c * NX + x] = ordered[:, k * BLK:(k + 1) * BLK]

    @pl.when(d == 0)
    def _():
        load_feat.wait()
        in_order(0, 1)

    pl.semaphore_wait(barrier, len(near) + rep)
    def remote(src, dst, sent, landed, target):
        return pltpu.make_async_remote_copy(
            src_ref=src, dst_ref=dst, send_sem=sent, recv_sem=landed, device_id=target, device_id_type=MESH
        )

    def copy_to(s, x0, kind, target):
        return remote(unit(s, x0), unit(s, x0), send_sem.at[kind], recv_sem.at[s, x0], target)

    def sib_sends(s, x0):
        ch = s // SUB
        whole = slabs.at[ch, c * NX + x0]

        @pl.when((s % SUB == SUB - 1) & (ch < CHUNKS - 1))
        def _():
            remote(whole, whole, send_sem.at[SIB], sib_sem.at[ch, x0], sibling).start()

        @pl.when(ch == CHUNKS - 1)
        def _():
            remote(unit(s, x0), unit(s, x0), send_sem.at[SIB], sib_sem.at[ch, x0], sibling).start()

    def sib_arrive(ch, x0):
        ref = slabs.at[ch, (1 - c) * NX + x0]
        remote(ref, ref, send_sem.at[SIB], sib_sem.at[ch, x0], sibling).wait_recv()

    second = (d == 2) | (d == NY - 2)

    half = CHUNKS // 2
    mine = pl.ds(c * half, half)

    def w_copy(k):
        ref = w_all.at[rep, mine]
        return remote(ref, ref, w_send, w_recv, (row, (rep + k) % NZ))

    def w_sib():
        ref = w_all.at[:, mine]
        return remote(ref, ref, w_sib_send, w_sib_recv, sibling)

    def own_step(s):
        even = (s + c) % 2 == 0
        for cond, kind, target in (
            ((d == 0) | ((d == 2) & even), YP2, up2),
            ((d == 0) | ((d == NY - 2) & jnp.logical_not(even)), YM2, down2),
            (second, YP1, up1),
            (second, YM1, down1),
        ):
            pl.when(cond)(copy_to(s, x, kind, target).start)
        copy_to(s, x, XP, right).start()
        copy_to(s, x, XM, left).start()
        pl.when(s >= DIRECT)(copy_to(s, x, XO, opposite).start)
        sib_sends(s, x)

    def arrive(s, x0):
        copy_to(s, x0, XP, right).wait_recv()

    def all_sent(kind, units):
        ref = slabs.at[0, :, pl.ds(0, units * (ROWS // (NC * NX)))]
        remote(ref, ref, send_sem.at[kind], w_recv, right).wait_send()

    def z_copy(ch, peer):
        return remote(z_out.at[ch, peer], z_in.at[ch, rep], z_send, z_recv.at[ch], (row, peer))

    @pl.when(d == 0)
    def _():
        def first(s, carry):
            own_step(s)
            return carry

        lax.fori_loop(0, PRE, first, 0)
        in_order(1, CHUNKS - 1)

    for k in range(1, NZ):
        @pl.when(rep >= k)
        def _(k=k):
            pl.semaphore_signal(ready, inc=1, device_id=(row, rep - k), device_id_type=MESH)

    load_w.wait()
    for k in (4, 3, 5, 2, 6, 1, 7):
        pl.when(rep + k >= NZ)(w_copy(k).start)

    adj[RB * NZ * KB] = jnp.zeros((BLK, BLK), jnp.bfloat16)
    load_cols.wait()
    load_count.wait()
    load_adj.wait()

    def build(jj, carry):
        j = (jj % NX) * NC + jj // NX
        for b in range(RB):
            cols = [cols_ref[k, b, j] for k in range(KB)]
            n = count_ref[b, j]
            base = (b * NZ + j) * KB
            for cb in range(RB):
                index = jnp.int32(RB * NZ * KB)
                for k in range(KB):
                    index = jnp.where((n > k) & (cols[k] == cb), base + k, index)
                dense[jj, b * BLK:(b + 1) * BLK, cb * BLK:(cb + 1) * BLK] = adj[index]
        return carry

    lax.fori_loop(0, NC * NX, build, 0)
    total[...] = jnp.zeros_like(total)

    def product(m, carry):
        ch, q = m // RB, m % RB

        from_left, from_right, across = (x + NX - 1) % NX, (x + 1) % NX, (x + 2) % NX
        x_a = jnp.where(q == 0, x, jnp.where(q == RB - 1, across, from_left))
        x_b = jnp.where(q == 0, x, jnp.where(q == RB - 1, across, from_right))

        @pl.when(q == 2)
        def _():
            sib_arrive(ch, x_a)

        @pl.when(q != 1)
        def _():
            sib_arrive(ch, x_b)

        a = jnp.where(q == 2, 1 - c, c) * NX + x_a
        b = jnp.where(q == 1, c, 1 - c) * NX + x_b
        update = jnp.dot(dense[a], slabs[ch, a], preferred_element_type=jnp.float32) + jnp.dot(
            dense[b], slabs[ch, b], preferred_element_type=jnp.float32
        )

        @pl.when(q == 0)
        def _():
            part[...] = update

        @pl.when(q > 0)
        def _():
            part[...] += update

        @pl.when(q == RB - 1)
        def _():
            initial = jnp.dot(perm[...], part[...].astype(jnp.bfloat16), preferred_element_type=jnp.float32)
            z_out[ch] = initial.astype(jnp.bfloat16).reshape(NZ, SLAB // NZ, BLK)
            for peer in range(NZ):
                pl.when(rep != peer)(z_copy(ch, peer).start)
            z_in[ch, rep] = z_out[ch, rep]

        return carry

    def iteration(i, carry):
        now = i + jnp.where(d == 0, PRE, 0)

        @pl.when((d != 0) & (i < STEPS))
        def _():
            arrive(i, x)

        @pl.when(now < STEPS)
        def _():
            own_step(now)

        @pl.when((i >= LAG_X1) & (i < STEPS + LAG_X1))
        def _():
            s = i - LAG_X1
            forward = s < DIRECT
            to_right = (s + c) % 2 == 0
            from_left, from_right = (x + NX - 1) % NX, (x + 1) % NX
            arrive(s, from_left)
            pl.when(forward & to_right)(copy_to(s, from_left, FR, right).start)
            sib_sends(s, from_left)
            arrive(s, from_right)
            pl.when(forward & jnp.logical_not(to_right))(copy_to(s, from_right, FL, left).start)
            sib_sends(s, from_right)

        @pl.when(i >= LAG_X2)
        def _():
            arrive(i - LAG_X2, (x + 2) % NX)
            sib_sends(i - LAG_X2, (x + 2) % NX)

        @pl.when(i == READY_AT)
        def _():
            @pl.when(rep < NZ - 1)
            def _():
                pl.semaphore_wait(ready, NZ - 1 - rep)

            for k in (4, 3, 5, 2, 6, 1, 7):
                pl.when(rep + k < NZ)(w_copy(k).start)

        @pl.when(i == WEIGHT_AT)
        def _():
            ref = w_all.at[pl.ds(0, NZ - 1), mine]
            remote(ref, ref, w_send, w_recv, sibling).wait()
            w_sib().start()

        @pl.when(i >= LAG_COMPUTE)
        def _():
            product(i - LAG_COMPUTE, 0)

        return carry

    lax.fori_loop(0, ITERS, iteration, 0)
    lax.fori_loop(ITERS - LAG_COMPUTE, CHUNKS * RB, product, 0)

    for kind, units in ((XP, STEPS), (XM, STEPS), (XO, STEPS - DIRECT)):
        all_sent(kind, units)
    for first, second_kind, core in ((FR, FL, 0), (FL, FR, 1)):
        @pl.when(c == core)
        def _(first=first, second_kind=second_kind):
            all_sent(first, (DIRECT + 1) // 2)
            all_sent(second_kind, DIRECT // 2)

    ref = slabs.at[:, pl.ds(0, NX)]
    remote(ref, ref, send_sem.at[SIB], w_recv, right).wait_send()

    @pl.when(d == 0)
    def _():
        all_sent(YP2, STEPS)
        all_sent(YM2, STEPS)

    @pl.when(second)
    def _():
        all_sent(YP1, STEPS)
        all_sent(YM1, STEPS)

    pl.when(d == 2)(functools.partial(all_sent, YP2, STEPS // 2))
    pl.when(d == NY - 2)(functools.partial(all_sent, YM2, STEPS // 2))
    w_sib().wait()

    def finish(ch, carry):
        ref = z_in.at[ch, pl.ds(0, NZ - 1)]
        remote(ref, ref, w_sib_send, z_recv.at[ch], sibling).wait_recv()
        rounded = jnp.sum(z_in[ch].astype(jnp.float32), axis=0).astype(jnp.bfloat16)
        for k in range(NZ):
            total[:, k * BLK:(k + 1) * BLK] += jnp.dot(rounded, w_all[k, ch], preferred_element_type=jnp.float32)
        return carry

    lax.fori_loop(0, CHUNKS, finish, 0)
    out_ref[...] = jnp.maximum(total[...], 0.0).astype(jnp.bfloat16)
    ref = z_out.at[:, pl.ds(0, NZ - 1)]
    remote(ref, ref, z_send, w_sib_recv, sibling).wait_send()


def shards(features, order, adj_values, adj_cols, adj_count, weight):
    hid = NZ * BLK
    bf16, f32, i32 = jnp.bfloat16, jnp.float32, jnp.int32
    dma = pltpu.SemaphoreType.DMA
    return pl.pallas_call(
        kernel,
        out_shape=jax.ShapeDtypeStruct((SLAB // NZ, hid), bf16),
        in_specs=[pl.BlockSpec(memory_space=pl.ANY)] * 6,
        out_specs=pl.BlockSpec(memory_space=pltpu.VMEM),
        scratch_shapes=[
            pltpu.VMEM((CHUNKS, NC * NX, SLAB, BLK), bf16),
            pltpu.VMEM((RB * NZ * KB + 1, BLK, BLK), bf16),
            pltpu.VMEM((NC * NX, SLAB, SLAB), bf16),
            pltpu.VMEM((SLAB, CHUNKS * BLK), bf16),
            pltpu.VMEM((SLAB, SLAB), bf16),
            pltpu.VMEM((1, SLAB), i32),
            pltpu.SMEM((KB, RB, NZ), i32),
            pltpu.SMEM((RB, NZ), i32),
            pltpu.VMEM((NZ, CHUNKS, BLK, BLK), bf16),
            pltpu.VMEM((SLAB, BLK), f32),
            pltpu.VMEM((CHUNKS, NZ, SLAB // NZ, BLK), bf16),
            pltpu.VMEM((CHUNKS, NZ, SLAB // NZ, BLK), bf16),
            pltpu.VMEM((SLAB // NZ, hid), f32),
            dma((6,)),
            dma((KINDS,)),
            dma((STEPS, NX)),
            dma((CHUNKS, NX)),
            dma,
            dma((CHUNKS,)),
            dma,
            dma,
            dma,
            dma,
            pltpu.SemaphoreType.REGULAR,
        ],
        compiler_params=pltpu.CompilerParams(
            collective_id=0, has_side_effects=True, vmem_limit_bytes=56 << 20
        ),
    )(
        features,
        order.reshape(1, SLAB),
        adj_values.reshape(RB * NZ * KB, BLK, BLK),
        adj_cols.transpose(2, 0, 1),
        adj_count,
        weight.reshape(CHUNKS, BLK, BLK),
    )


def solution(mesh):
    placed = (
        P("row", None),
        P("row"),
        P("row", "rep", None, None, None),
        P("row", "rep", None),
        P("row", "rep"),
        P(None, "rep"),
    )
    return jax.shard_map(
        shards, mesh=mesh, in_specs=placed, out_specs=P(("row", "rep"), None), check_vma=False
    )
```

```python
import functools

import jax
import jax.numpy as jnp
from jax import lax
from jax.experimental import pallas as pl
from jax.experimental.pallas import tpu as pltpu
from jax.sharding import PartitionSpec as P

MESH = pl.DeviceIdType.MESH
NY, NX, NC, NZ = 8, 4, 2, 8
BLK = 128
RB = 4
KB = 3
SLAB = RB * BLK
CHUNKS = 6
SUB = 4
ROWS = SLAB // SUB
STEPS = CHUNKS * SUB
PRE = 4
LAG_X1 = 4
LAG_X2 = 8
LAG_COMPUTE = 10
ITERS = LAG_X2 + STEPS
DIRECT = STEPS - 1
READY_AT = 4
WEIGHT_AT = 29
YP1, YM1, YP2, YM2, XP, XM, XO, FR, FL, SIB = range(10)
KINDS = SIB + 1


def kernel(
    feat_hbm, order_hbm, adj_hbm, cols_hbm, count_hbm, w_hbm, out_ref,
    slabs, adj, dense, feat, perm, order, cols_ref, count_ref, w_all, part, z_out, z_in, total,
    load_sem, send_sem, recv_sem, sib_sem, z_send, z_recv, w_send, w_recv, w_sib_send, w_sib_recv, ready,
):
    row = lax.axis_index("row")
    rep = lax.axis_index("rep")
    c = row % NC
    x = (row // NC) % NX
    y = row // (NC * NX)
    d = (y - rep + NY) % NY

    def device(dy, dx, dc):
        return ((((y + dy) % NY) * NX + (x + dx) % NX) * NC + (c + dc) % NC, rep)

    left, right, opposite, sibling = device(0, NX - 1, 0), device(0, 1, 0), device(0, 2, 0), device(0, 0, 1)
    up1, down1, up2, down2 = device(1, 0, 0), device(NY - 1, 0, 0), device(2, 0, 0), device(NY - 2, 0, 0)

    barrier = pltpu.get_barrier_semaphore()
    near = (left, right, opposite, sibling, up1, down1, up2, down2)
    for other in near:
        pl.semaphore_signal(barrier, inc=1, device_id=other, device_id_type=MESH)
    for k in range(1, NZ):
        @pl.when(rep + k < NZ)
        def _(k=k):
            pl.semaphore_signal(barrier, inc=1, device_id=(row, rep + k), device_id_type=MESH)

    load_order = pltpu.make_async_copy(order_hbm, order, load_sem.at[0])
    load_feat = pltpu.make_async_copy(feat_hbm, feat, load_sem.at[1])
    load_adj = pltpu.make_async_copy(adj_hbm, adj.at[pl.ds(0, RB * NZ * KB)], load_sem.at[2])
    load_cols = pltpu.make_async_copy(cols_hbm, cols_ref, load_sem.at[3])
    load_count = pltpu.make_async_copy(count_hbm, count_ref, load_sem.at[4])
    load_w = pltpu.make_async_copy(w_hbm, w_all.at[rep], load_sem.at[5])
    load_order.start()

    @pl.when(d == 0)
    def _():
        load_feat.start()

    load_adj.start()
    load_cols.start()
    load_count.start()
    load_w.start()
    load_order.wait()
    local = order[...] - row * SLAB
    rows_of = lax.broadcasted_iota(jnp.int32, (SLAB, SLAB), 0)
    perm[...] = (rows_of == local).astype(jnp.float32).astype(jnp.bfloat16)

    def unit(s, x0):
        return slabs.at[s // SUB, c * NX + x0, pl.ds((s % SUB) * ROWS, ROWS)]

    def in_order(first, count):
        ordered = lax.dot_general(
            perm[...], feat[:, first * BLK:(first + count) * BLK], (((0,), (0,)), ((), ())),
            preferred_element_type=jnp.float32,
        ).astype(jnp.bfloat16)
        for k in range(count):
            slabs[first + k, c * NX + x] = ordered[:, k * BLK:(k + 1) * BLK]

    @pl.when(d == 0)
    def _():
        load_feat.wait()
        in_order(0, 1)

    pl.semaphore_wait(barrier, len(near) + rep)
    def remote(src, dst, sent, landed, target):
        return pltpu.make_async_remote_copy(
            src_ref=src, dst_ref=dst, send_sem=sent, recv_sem=landed, device_id=target, device_id_type=MESH
        )

    def copy_to(s, x0, kind, target):
        return remote(unit(s, x0), unit(s, x0), send_sem.at[kind], recv_sem.at[s, x0], target)

    def sib_sends(s, x0):
        ch = s // SUB
        whole = slabs.at[ch, c * NX + x0]

        @pl.when((s % SUB == SUB - 1) & (ch < CHUNKS - 1))
        def _():
            remote(whole, whole, send_sem.at[SIB], sib_sem.at[ch, x0], sibling).start()

        @pl.when(ch == CHUNKS - 1)
        def _():
            remote(unit(s, x0), unit(s, x0), send_sem.at[SIB], sib_sem.at[ch, x0], sibling).start()

    def sib_arrive(ch, x0):
        ref = slabs.at[ch, (1 - c) * NX + x0]
        remote(ref, ref, send_sem.at[SIB], sib_sem.at[ch, x0], sibling).wait_recv()

    second = (d == 2) | (d == NY - 2)

    half = CHUNKS // 2
    mine = pl.ds(c * half, half)

    def w_copy(k):
        ref = w_all.at[rep, mine]
        return remote(ref, ref, w_send, w_recv, (row, (rep + k) % NZ))

    def w_sib():
        ref = w_all.at[:, mine]
        return remote(ref, ref, w_sib_send, w_sib_recv, sibling)

    def own_step(s):
        even = (s + c) % 2 == 0
        for cond, kind, target in (
            ((d == 0) | ((d == 2) & even), YP2, up2),
            ((d == 0) | ((d == NY - 2) & jnp.logical_not(even)), YM2, down2),
            (second, YP1, up1),
            (second, YM1, down1),
        ):
            pl.when(cond)(copy_to(s, x, kind, target).start)
        copy_to(s, x, XP, right).start()
        copy_to(s, x, XM, left).start()
        pl.when(s >= DIRECT)(copy_to(s, x, XO, opposite).start)
        sib_sends(s, x)

    def arrive(s, x0):
        copy_to(s, x0, XP, right).wait_recv()

    def all_sent(kind, units):
        ref = slabs.at[0, :, pl.ds(0, units * (ROWS // (NC * NX)))]
        remote(ref, ref, send_sem.at[kind], w_recv, right).wait_send()

    def z_copy(ch, peer):
        return remote(z_out.at[ch, peer], z_in.at[ch, rep], z_send, z_recv.at[ch], (row, peer))

    @pl.when(d == 0)
    def _():
        def first(s, carry):
            own_step(s)
            return carry

        lax.fori_loop(0, PRE, first, 0)
        in_order(1, CHUNKS - 1)

    for k in range(1, NZ):
        @pl.when(rep >= k)
        def _(k=k):
            pl.semaphore_signal(ready, inc=1, device_id=(row, rep - k), device_id_type=MESH)

    load_w.wait()
    for k in (4, 3, 5, 2, 6, 1, 7):
        pl.when(rep + k >= NZ)(w_copy(k).start)

    adj[RB * NZ * KB] = jnp.zeros((BLK, BLK), jnp.bfloat16)
    load_cols.wait()
    load_count.wait()
    load_adj.wait()

    def build(jj, carry):
        j = (jj % NX) * NC + jj // NX
        for b in range(RB):
            cols = [cols_ref[k, b, j] for k in range(KB)]
            n = count_ref[b, j]
            base = (b * NZ + j) * KB
            for cb in range(RB):
                index = jnp.int32(RB * NZ * KB)
                for k in range(KB):
                    index = jnp.where((n > k) & (cols[k] == cb), base + k, index)
                dense[jj, b * BLK:(b + 1) * BLK, cb * BLK:(cb + 1) * BLK] = adj[index]
        return carry

    lax.fori_loop(0, NC * NX, build, 0)
    total[...] = jnp.zeros_like(total)

    def product(m, carry):
        ch, q = m // RB, m % RB

        from_left, from_right, across = (x + NX - 1) % NX, (x + 1) % NX, (x + 2) % NX
        x_a = jnp.where(q == 0, x, jnp.where(q == RB - 1, across, from_left))
        x_b = jnp.where(q == 0, x, jnp.where(q == RB - 1, across, from_right))

        @pl.when(q == 2)
        def _():
            sib_arrive(ch, x_a)

        @pl.when(q != 1)
        def _():
            sib_arrive(ch, x_b)

        a = jnp.where(q == 2, 1 - c, c) * NX + x_a
        b = jnp.where(q == 1, c, 1 - c) * NX + x_b
        update = jnp.dot(dense[a], slabs[ch, a], preferred_element_type=jnp.float32) + jnp.dot(
            dense[b], slabs[ch, b], preferred_element_type=jnp.float32
        )

        @pl.when(q == 0)
        def _():
            part[...] = update

        @pl.when(q > 0)
        def _():
            part[...] += update

        @pl.when(q == RB - 1)
        def _():
            initial = jnp.dot(perm[...], part[...].astype(jnp.bfloat16), preferred_element_type=jnp.float32)
            z_out[ch] = initial.astype(jnp.bfloat16).reshape(NZ, SLAB // NZ, BLK)
            for peer in range(NZ):
                pl.when(rep != peer)(z_copy(ch, peer).start)
            z_in[ch, rep] = z_out[ch, rep]

        return carry

    def iteration(i, carry):
        now = i + jnp.where(d == 0, PRE, 0)

        @pl.when((d != 0) & (i < STEPS))
        def _():
            arrive(i, x)

        @pl.when(now < STEPS)
        def _():
            own_step(now)

        @pl.when((i >= LAG_X1) & (i < STEPS + LAG_X1))
        def _():
            s = i - LAG_X1
            forward = s < DIRECT
            to_right = (s + c) % 2 == 0
            from_left, from_right = (x + NX - 1) % NX, (x + 1) % NX
            arrive(s, from_left)
            pl.when(forward & to_right)(copy_to(s, from_left, FR, right).start)
            sib_sends(s, from_left)
            arrive(s, from_right)
            pl.when(forward & jnp.logical_not(to_right))(copy_to(s, from_right, FL, left).start)
            sib_sends(s, from_right)

        @pl.when(i >= LAG_X2)
        def _():
            arrive(i - LAG_X2, (x + 2) % NX)
            sib_sends(i - LAG_X2, (x + 2) % NX)

        @pl.when(i == READY_AT)
        def _():
            @pl.when(rep < NZ - 1)
            def _():
                pl.semaphore_wait(ready, NZ - 1 - rep)

            for k in (4, 3, 5, 2, 6, 1, 7):
                pl.when(rep + k < NZ)(w_copy(k).start)

        @pl.when(i == WEIGHT_AT)
        def _():
            ref = w_all.at[pl.ds(0, NZ - 1), mine]
            remote(ref, ref, w_send, w_recv, sibling).wait()
            w_sib().start()

        @pl.when(i >= LAG_COMPUTE)
        def _():
            product(i - LAG_COMPUTE, 0)

        return carry

    lax.fori_loop(0, ITERS, iteration, 0)
    lax.fori_loop(ITERS - LAG_COMPUTE, CHUNKS * RB, product, 0)

    for kind, units in ((XP, STEPS), (XM, STEPS), (XO, STEPS - DIRECT)):
        all_sent(kind, units)
    for first, second_kind, core in ((FR, FL, 0), (FL, FR, 1)):
        @pl.when(c == core)
        def _(first=first, second_kind=second_kind):
            all_sent(first, (DIRECT + 1) // 2)
            all_sent(second_kind, DIRECT // 2)

    ref = slabs.at[:, pl.ds(0, NX)]
    remote(ref, ref, send_sem.at[SIB], w_recv, right).wait_send()

    @pl.when(d == 0)
    def _():
        all_sent(YP2, STEPS)
        all_sent(YM2, STEPS)

    @pl.when(second)
    def _():
        all_sent(YP1, STEPS)
        all_sent(YM1, STEPS)

    pl.when(d == 2)(functools.partial(all_sent, YP2, STEPS // 2))
    pl.when(d == NY - 2)(functools.partial(all_sent, YM2, STEPS // 2))
    w_sib().wait()

    def finish(ch, carry):
        ref = z_in.at[ch, pl.ds(0, NZ - 1)]
        remote(ref, ref, w_sib_send, z_recv.at[ch], sibling).wait_recv()
        rounded = jnp.sum(z_in[ch].astype(jnp.float32), axis=0).astype(jnp.bfloat16)
        for k in range(NZ):
            total[:, k * BLK:(k + 1) * BLK] += jnp.dot(rounded, w_all[k, ch], preferred_element_type=jnp.float32)
        return carry

    lax.fori_loop(0, CHUNKS, finish, 0)
    out_ref[...] = jnp.maximum(total[...], 0.0).astype(jnp.bfloat16)
    ref = z_out.at[:, pl.ds(0, NZ - 1)]
    remote(ref, ref, z_send, w_sib_recv, sibling).wait_send()


def shards(features, order, adj_values, adj_cols, adj_count, weight):
    hid = NZ * BLK
    bf16, f32, i32 = jnp.bfloat16, jnp.float32, jnp.int32
    dma = pltpu.SemaphoreType.DMA
    return pl.pallas_call(
        kernel,
        out_shape=jax.ShapeDtypeStruct((SLAB // NZ, hid), bf16),
        in_specs=[pl.BlockSpec(memory_space=pl.ANY)] * 6,
        out_specs=pl.BlockSpec(memory_space=pltpu.VMEM),
        scratch_shapes=[
            pltpu.VMEM((CHUNKS, NC * NX, SLAB, BLK), bf16),
            pltpu.VMEM((RB * NZ * KB + 1, BLK, BLK), bf16),
            pltpu.VMEM((NC * NX, SLAB, SLAB), bf16),
            pltpu.VMEM((SLAB, CHUNKS * BLK), bf16),
            pltpu.VMEM((SLAB, SLAB), bf16),
            pltpu.VMEM((1, SLAB), i32),
            pltpu.SMEM((KB, RB, NZ), i32),
            pltpu.SMEM((RB, NZ), i32),
            pltpu.VMEM((NZ, CHUNKS, BLK, BLK), bf16),
            pltpu.VMEM((SLAB, BLK), f32),
            pltpu.VMEM((CHUNKS, NZ, SLAB // NZ, BLK), bf16),
            pltpu.VMEM((CHUNKS, NZ, SLAB // NZ, BLK), bf16),
            pltpu.VMEM((SLAB // NZ, hid), f32),
            dma((6,)),
            dma((KINDS,)),
            dma((STEPS, NX)),
            dma((CHUNKS, NX)),
            dma,
            dma((CHUNKS,)),
            dma,
            dma,
            dma,
            dma,
            pltpu.SemaphoreType.REGULAR,
        ],
        compiler_params=pltpu.CompilerParams(
            collective_id=0, has_side_effects=True, vmem_limit_bytes=56 << 20
        ),
    )(
        features,
        order.reshape(1, SLAB),
        adj_values.reshape(RB * NZ * KB, BLK, BLK),
        adj_cols.transpose(2, 0, 1),
        adj_count,
        weight.reshape(CHUNKS, BLK, BLK),
    )


def solution(mesh):
    placed = (
        P("row", None),
        P("row"),
        P("row", "rep", None, None, None),
        P("row", "rep", None),
        P("row", "rep"),
        P(None, "rep"),
    )
    return jax.shard_map(
        shards, mesh=mesh, in_specs=placed, out_specs=P(("row", "rep"), None), check_vma=False
    )
```
